32 devices in a mesh: groups: 2 (over x), dom: 16 (over z, y, core).
Axes of the slice: x: 2, y: 2, z: 4, core: 2. Of those that a mesh axis runs over, the one named last changes fastest.
Arguments:
- adjoint_start: float32 [6, 128, 64, 128], P(None, None, ('groups', 'dom')), parts along dimension 2, may hold values from -6 to 6
- source: float32 [6, 128, 64, 128], P(None, None, ('groups', 'dom')), parts along dimension 2, may hold values from -6 to 6
- state: bfloat16 [6, 128, 64, 128], P(None, None, ('groups', 'dom')), parts along dimension 2, may hold values from -0.4 to 4, as said below
- pseudo_step: float32 [128, 64, 128], P(None, ('groups', 'dom')), parts along dimension 1, may hold values from 0.04 to 0.16
- row_counts: int32 [12], P('groups'), parts along dimension 0, may hold values from 1 to 8, as said below
Outputs:
- adjoint: float32 [6, 128, 64, 128], P(None, None, ('groups', 'dom')), parts along dimension 2
The draws below stay inside these ranges and needn't reach their ends.
There are 2 independent parts, one for each index of `groups`. The reference program is written for one: setup_inputs(seed, part) draws one part's arguments, and reference() takes and returns one part's arrays. A program takes and returns all parts, laid end to end along the dimension named above; each array names one. Nothing has to cross between parts.
Inputs may be any that keep to these rules, and one draw needn't show every extreme that they name: `state`: component 0 (density) lies in 0.7 to 1.3, components 1 to 3 (momenta) in -0.4 to 0.4, component 5 in 0.5 to 2, and the pressure 0.4 (e - 0.5 |m|^2 / density) of every cell in 0.6 to 1.4. `row_counts`: the counts sum to 16; every row holds at least 1 block, and one row holds exactly 8.
All inputs are finite; a program needn't handle non-finite values.
Results may differ from the reference program's by a relative error of at most 0.0003.
Values may be sent and summed in bfloat16 or wider, within the bound.
A program may use at most 64 MiB of HBM per device.

```python
import math
import jax
import jax.numpy as jnp
from jax import lax

COMPS = 6
PITCH = 128
AXIAL = 128
RAD_DEV = 2
BANDS = 256
ROWS = 6
ITERS = 2
RADIAL = 32
N_DOM = 16


def draw_state(key, part):
    key = jax.random.fold_in(key, 11)
    keys = jax.random.split(key, 4)
    shape = (PITCH, RADIAL, AXIAL)
    density = jax.random.uniform(keys[0], shape, jnp.float32, 0.7, 1.3)
    momentum = jax.random.uniform(keys[1], (3,) + shape, jnp.float32, -0.39, 0.39)
    pressure = jax.random.uniform(keys[2], shape, jnp.float32, 0.6, 1.4)
    viscous = jax.random.uniform(keys[3], shape, jnp.float32, 0.5, 2.0)
    energy = pressure / 0.4 + 0.5 * jnp.sum(momentum * momentum, axis=0) / density
    flow = jnp.concatenate([density[None], momentum, energy[None], viscous[None]], axis=0)
    return flow.astype(jnp.bfloat16)


def draw_adjoint_start(key, part):
    key = jax.random.fold_in(key, 5)
    keys = jax.random.split(key, 2)
    shape = (COMPS, PITCH, RADIAL, AXIAL)
    noise = jax.random.truncated_normal(keys[0], -4.0, 4.0, shape, jnp.float32)
    radial_part = jax.random.uniform(keys[1], (COMPS, 1, RADIAL, AXIAL), jnp.float32, -1.5, 1.5)
    field = noise + radial_part
    return field.astype(jnp.float32)


def draw_row_counts(key, part):
    key = jax.random.fold_in(key, 23)
    keys = jax.random.split(key, 4)
    most = N_DOM // 2
    least = N_DOM // 16
    others = ROWS - 1
    extra = N_DOM - most - others * least
    room = most - least
    base = extra // others
    spare = extra - base * others
    shares = jnp.full((others,), base, jnp.int32) + (jnp.arange(others, dtype=jnp.int32) < spare).astype(jnp.int32)
    order = jax.random.permutation(keys[0], others)
    limit = min(base, room - base - 1) + 1
    first_move = jax.random.randint(keys[1], (), 0, limit, jnp.int32)
    shares = shares.at[order[0]].add(-first_move).at[order[1]].add(first_move)
    second_move = jax.random.randint(keys[2], (), 0, limit, jnp.int32)
    shares = shares.at[order[2]].add(-second_move).at[order[3]].add(second_move)
    counts = jnp.concatenate([jnp.full((1,), most, jnp.int32), least + shares])
    return jax.random.permutation(keys[3], counts).astype(jnp.int32)


def steps_of(own_key, extent, cuts, low, top_value):
    def one(dim, shards_of):
        heights = jax.random.uniform(jax.random.fold_in(jax.random.fold_in(own_key, 6), dim), (shards_of,), jnp.float32, low / len(cuts), top_value / len(cuts))
        return jnp.repeat(jnp.exp(heights), extent[dim] // shards_of).reshape((-1,) + (1,) * (len(extent) - dim - 1))

    factor_of = one(*cuts[0])
    for cut in cuts[1:]:
        factor_of = factor_of * one(*cut)
    return factor_of


def gaussian(key, dims, scale, reach, shards=(), kind=jnp.bfloat16):
    drawn = scale * jax.random.normal(key, dims, jnp.float32)
    if shards:
        drawn = drawn * steps_of(key, dims, shards, -0.22, 0.18)
    return jnp.clip(drawn, -reach, reach).astype(kind)


def setup_inputs(seed: int = 0, part: int = 0) -> dict:
    seeds = jax.random.split(jax.random.key(seed), 6)
    part_keys = jax.random.split(jax.random.fold_in(seeds[5], part), 6)
    adjoint_start = draw_adjoint_start(jax.random.fold_in(jax.random.fold_in(seeds[5], part), 71), part)
    source = gaussian(part_keys[1], (COMPS, PITCH, RADIAL, AXIAL), 1.0, 6.0, ((2, 16),), jnp.float32)
    state = draw_state(jax.random.fold_in(jax.random.fold_in(seeds[5], part), 71), part)
    pseudo_step = jnp.clip(jnp.exp(math.log(0.16) - 1.3862944 * jax.random.uniform(part_keys[3], (PITCH, RADIAL, AXIAL), jnp.float32) ** steps_of(part_keys[3], (PITCH, RADIAL, AXIAL), ((1, 16),), -0.2, 0.2)), 0.04, 0.16)
    row_counts = draw_row_counts(jax.random.fold_in(jax.random.fold_in(seeds[5], part), 71), part)
    return {"adjoint_start": adjoint_start, "source": source, "state": state, "pseudo_step": pseudo_step, "row_counts": row_counts}


damping = 2.0

def fluxes(flow):
    density = flow[0]
    momentum = flow[1:4]
    energy = flow[4]
    viscous = flow[5]
    velocity = momentum / density
    pressure = 0.4 * (energy - 0.5 * lax.optimization_barrier(jnp.sum(momentum * velocity, axis=0)))
    result = []
    for direction in range(3):
        parts = [momentum[direction]]
        for other in range(3):
            term = momentum[other] * velocity[direction]
            if other == direction:
                term = term + pressure
            parts.append(term)
        parts.append(velocity[direction] * (energy + pressure))
        parts.append(velocity[direction] * viscous)
        result.append(jnp.stack(parts))
    return tuple(result)

def transposed(centre, below_side, above_side, inlet_ghost, outlet_ghost, flow):
    pitch_minus = jnp.roll(centre, 1, axis=1)
    pitch_plus = jnp.roll(centre, -1, axis=1)
    axial_minus = jnp.concatenate([inlet_ghost, centre[..., :-1]], axis=3)
    axial_plus = jnp.concatenate([centre[..., 1:], outlet_ghost], axis=3)
    cotangent = (0.5 * (pitch_minus - pitch_plus), 0.5 * (below_side - above_side), 0.5 * (axial_minus - axial_plus))
    unused, pullback = jax.vjp(fluxes, flow)
    convected = pullback(cotangent)[0]
    spread = 6.0 * centre - pitch_minus - pitch_plus - below_side - above_side - axial_minus - axial_plus
    return convected + 0.5 * damping * spread

def intersection(position, row_cells):
    band_ids = jnp.arange(BANDS, dtype=jnp.int32)[None, :]
    low_end = jnp.maximum(position[:, None] * BANDS, band_ids * row_cells[:, None])
    high_end = jnp.minimum((position[:, None] + 1) * BANDS, (band_ids + 1) * row_cells[:, None])
    return jnp.maximum(high_end - low_end, 0).astype(jnp.float32)

def reference(adjoint_start, source, state, pseudo_step, row_counts):
    row_ends = jnp.cumsum(row_counts).astype(jnp.int32)
    row_starts = row_ends - row_counts
    cell_ids = jnp.arange(RADIAL, dtype=jnp.int32)
    owner = cell_ids // RAD_DEV
    cell_row = lax.optimization_barrier(jnp.sum((owner[:, None] >= row_ends[None, :]).astype(jnp.int32), axis=1))
    position = cell_ids - row_starts[cell_row] * RAD_DEV
    row_cells = row_counts[cell_row] * RAD_DEV
    weights = intersection(position, row_cells)
    row_ids = jnp.arange(ROWS, dtype=jnp.int32)[None, :]
    own_select = (cell_row[:, None] == row_ids).astype(jnp.float32)
    prev_select = (cell_row[:, None] - 1 == row_ids).astype(jnp.float32)
    next_select = (cell_row[:, None] + 1 == row_ids).astype(jnp.float32)
    scaled = weights / (PITCH * row_cells).astype(jnp.float32)[:, None]
    flow = state.astype(jnp.float32)
    below_ok = (position >= 1)[None, None, :, None]
    above_ok = (position + 1 < row_cells)[None, None, :, None]
    highest = lax.Precision.HIGHEST
    adjoint = adjoint_start
    for sweep_index in range(ITERS):
        sums_in = lax.optimization_barrier(jnp.sum(adjoint[..., 0], axis=1))
        sums_out = lax.optimization_barrier(jnp.sum(adjoint[..., -1], axis=1))
        table_in = jnp.einsum('gr,cg,gb->rcb', own_select, sums_in, scaled, precision=highest)
        table_out = jnp.einsum('gr,cg,gb->rcb', own_select, sums_out, scaled, precision=highest)
        inlet_vals = jnp.einsum('gr,rcb,gb->cg', prev_select, table_out, weights, precision=highest) / BANDS
        outlet_vals = jnp.einsum('gr,rcb,gb->cg', next_select, table_in, weights, precision=highest) / BANDS
        inlet_ghost = jnp.broadcast_to(inlet_vals[:, None, :, None], (COMPS, PITCH, RADIAL, 1))
        outlet_ghost = jnp.broadcast_to(outlet_vals[:, None, :, None], (COMPS, PITCH, RADIAL, 1))
        padded = jnp.pad(adjoint, ((0, 0), (0, 0), (1, 1), (0, 0)))
        below_side = jnp.where(below_ok, padded[:, :, :-2], 0.0)
        above_side = jnp.where(above_ok, padded[:, :, 2:], 0.0)
        image = transposed(adjoint, below_side, above_side, inlet_ghost, outlet_ghost, flow)
        adjoint = adjoint - pseudo_step[None] * (image - source)
    return adjoint
```

```python
import functools

import jax
import jax.numpy as jnp
from jax import lax
from jax.experimental import pallas as pl
from jax.experimental.pallas import tpu as pltpu
from jax.sharding import PartitionSpec as P

BANDS = 256
ROWS = 6
SWEEPS = 2
LANES = 128
PAD = 8
GROUP = 16
MESH = pl.DeviceIdType.MESH
HALO = jnp.float32


def total(parts):
    result = parts[0]
    for part in parts[1:]:
        result = result + part
    return result


def update(c, pm, pp, lo, hi, am, ap, prim, source, step):
    v, enthalpy, ratio, kinetic = prim[:3], prim[3], prim[4], prim[5]
    comps = range(len(c))
    a = [
        [pm[i] - pp[i] for i in comps],
        [lo[i] - hi[i] for i in comps],
        [am[i] - ap[i] for i in comps],
    ]
    by_velocity = [
        total([a[d][1 + k] * v[k] for k in range(3)]) + a[d][4] * enthalpy + a[d][5] * ratio
        for d in range(3)
    ]
    energy = total([a[d][4] * v[d] for d in range(3)])
    by_pressure = a[0][1] + a[1][2] + a[2][3] + energy
    scaled = 0.4 * by_pressure
    convected = [kinetic * by_pressure - total([v[d] * by_velocity[d] for d in range(3)])]
    for k in range(3):
        convected.append(
            a[k][0]
            + total([a[d][1 + k] * v[d] for d in range(3)])
            - v[k] * scaled
            + by_velocity[k]
        )
    convected.append(energy + scaled)
    convected.append(total([a[d][5] * v[d] for d in range(3)]))
    result = []
    for i in comps:
        around = (pm[i] + pp[i]) + (lo[i] + hi[i]) + (am[i] + ap[i])
        image = 0.5 * convected[i] + (6.0 * c[i] - around)
        result.append(c[i] - step * (image - source[i]))
    return result


def kernel(
    n, comps, pitch, chunks,
    counts, adj_in, src_in, st_in, ps_in, out,
    adj, src, st, ps, prim, mid, fin,
    snd_dn, snd_up, rcv_lo, rcv_hi, gsend, gath, ghost, weight,
    load_sem, store_sem, dn_send, dn_recv, up_send, up_recv, g_send, g_recv,
):
    cells = 2 * pitch
    span = pitch // chunks
    me = lax.axis_index("dom")
    f32 = jnp.float32

    loads = [
        pltpu.make_async_copy(adj_in, adj.at[:, pl.ds(PAD, cells), :], load_sem.at[0]),
        pltpu.make_async_copy(st_in, st, load_sem.at[1]),
        pltpu.make_async_copy(src_in, src, load_sem.at[2]),
        pltpu.make_async_copy(ps_in, ps, load_sem.at[3]),
    ]
    for load in loads:
        load.start()

    barrier = pltpu.get_barrier_semaphore()
    for k in range(1, n):
        pl.semaphore_signal(
            barrier, inc=1, device_id={"dom": lax.rem(me + k, n)}, device_id_type=MESH
        )

    lane = lax.broadcasted_iota(jnp.int32, (1, LANES), 1)

    starts, ends = [], []
    end = jnp.int32(0)
    for r in range(ROWS):
        starts.append(end)
        end = end + counts[r]
        ends.append(end)

    def placed(dev):
        row = total([(dev >= e).astype(jnp.int32) for e in ends])
        start = jnp.zeros_like(row)
        count = jnp.zeros_like(row)
        for r in range(ROWS):
            start = jnp.where(row == r, starts[r], start)
            count = jnp.where(row == r, counts[r], count)
        return row, start, count

    band = lax.broadcasted_iota(jnp.int32, (1, BANDS), 1)

    def overlap(position, row_cells):
        low = jnp.maximum(position * BANDS, band * row_cells)
        high = jnp.minimum((position + 1) * BANDS, (band + 1) * row_cells)
        return jnp.maximum(high - low, 0).astype(f32)

    mine = jnp.full((1, 1), me, jnp.int32)
    my_row, my_start, my_count = placed(mine)
    dev = me - lax.broadcasted_iota(jnp.int32, (n, 1), 0)
    dev = jnp.where(dev < 0, dev + n, dev)
    row, start, count = placed(dev)
    from_next = (row == my_row + 1).astype(f32)
    from_prev = (row == my_row - 1).astype(f32)
    own = [overlap(2 * (mine - my_start) + i, 2 * my_count) for i in range(2)]
    theirs = [overlap(2 * (dev - start) + r, 2 * count) for r in range(2)]
    scale = 1.0 / (pitch * BANDS * 2 * count).astype(f32)
    for i in range(2):
        dots = [jnp.sum(theirs[r] * own[i], axis=1, keepdims=True) * scale for r in range(2)]
        weight[i] = jnp.where(
            lane < 8, from_next * dots[0],
            jnp.where(
                lane < 16, from_next * dots[1],
                jnp.where(
                    lane < 24, from_prev * dots[0],
                    jnp.where(lane < 32, from_prev * dots[1], 0.0),
                ),
            ),
        )

    place = jnp.zeros((1, LANES), jnp.int32) + (mine - my_start)
    below_ok = place > 0
    above_ok = place + 1 < my_count

    def send_sums(sweep, sums):
        message = jnp.zeros((1, LANES), f32)
        for r in range(2):
            for c in range(comps):
                whole = jnp.sum(sums[r][c], axis=0, keepdims=True)
                at = c + 8 * r
                message = jnp.where(lane == at, pltpu.roll(whole, at, 1) if at else whole, message)
                message = jnp.where(lane == at + 16, pltpu.roll(whole, at + 17, 1), message)
        gsend[sweep] = message
        gath[sweep, 0] = message

    def sums_copy(sweep, k):
        return pltpu.make_async_remote_copy(
            src_ref=gsend.at[sweep],
            dst_ref=gath.at[sweep, k],
            send_sem=g_send.at[sweep, k],
            recv_sem=g_recv.at[sweep, k],
            device_id={"dom": lax.rem(me + k, n)},
            device_id_type=MESH,
        )

    def down_copy(sweep, ch):
        return pltpu.make_async_remote_copy(
            src_ref=snd_dn.at[sweep, ch],
            dst_ref=rcv_hi.at[sweep, ch],
            send_sem=dn_send.at[sweep, ch],
            recv_sem=dn_recv.at[sweep, ch],
            device_id={"dom": jnp.maximum(me - 1, 0)},
            device_id_type=MESH,
        )

    def up_copy(sweep, ch):
        return pltpu.make_async_remote_copy(
            src_ref=snd_up.at[sweep, ch],
            dst_ref=rcv_lo.at[sweep, ch],
            send_sem=up_send.at[sweep, ch],
            recv_sem=up_recv.at[sweep, ch],
            device_id={"dom": jnp.minimum(me + 1, n - 1)},
            device_id_type=MESH,
        )

    def send_halo(sweep, ch):
        @pl.when(me > 0)
        def _():
            down_copy(sweep, ch).start()

        @pl.when(me < n - 1)
        def _():
            up_copy(sweep, ch).start()

    def wrap(field):
        field[:, PAD - 2 : PAD, :] = field[:, PAD + cells - 2 : PAD + cells, :]
        field[:, PAD + cells : PAD + cells + 2, :] = field[:, PAD : PAD + 2, :]

    zero_sums = tuple(jnp.zeros((8, LANES), f32) for _ in range(2 * comps))

    def added(sums, r, values):
        sums = list(sums)
        for c in range(comps):
            for part in range(GROUP // 8):
                sums[r * comps + c] = sums[r * comps + c] + values[c][8 * part : 8 * part + 8]
        return tuple(sums)

    def split(sums):
        return [sums[:comps], sums[comps:]]

    loads[0].wait()

    def first(ch, sums):
        for part in range(span // GROUP):
            at = pl.multiple_of(PAD + 2 * (ch * span + part * GROUP), 8)
            for r in range(2):
                values = [
                    adj[c, pl.ds(at + r, GROUP, stride=2), :] for c in range(comps)
                ]
                target = (snd_dn, snd_up)[r]
                for c in range(comps):
                    target[0, ch, c, part * GROUP : (part + 1) * GROUP, :] = values[c].astype(HALO)
                sums = added(sums, r, values)
        return sums

    sums = lax.fori_loop(0, chunks, first, zero_sums)
    send_sums(0, split(sums))
    pl.semaphore_wait(barrier, n - 1)
    for k in range(1, n):
        sums_copy(0, k).start()

    def send_first(ch, carry):
        send_halo(0, ch)
        return carry

    lax.fori_loop(0, chunks, send_first, 0)
    wrap(adj)

    loads[1].wait()

    def primitive(j, carry):
        at = pl.ds(pl.multiple_of(j * 16, 16), 16)
        flow = [st[c, at, :].astype(f32) for c in range(6)]
        inverse = 1.0 / flow[0]
        v = [flow[1 + d] * inverse for d in range(3)]
        kinetic = 0.5 * total([flow[1 + d] * v[d] for d in range(3)])
        pressure = 0.4 * (flow[4] - kinetic)
        values = v + [(flow[4] + pressure) * inverse, flow[5] * inverse, 0.4 * kinetic * inverse]
        for c in range(6):
            prim[c, at, :] = values[c]
        return carry

    lax.fori_loop(0, cells // 16, primitive, 0)
    loads[2].wait()
    loads[3].wait()

    for sweep in range(SWEEPS):
        last = sweep == SWEEPS - 1
        old = adj if sweep == 0 else mid
        for k in range(1, n):
            sums_copy(sweep, k).wait_recv()
        gathered = gath[sweep][:, 0, :]
        for i in range(2):
            mixed = jnp.sum(weight[i] * gathered, axis=0, keepdims=True)
            mixed = mixed + pltpu.roll(mixed, LANES - 8, 1)
            for c in range(comps):
                ghost[sweep, i, c] = jnp.where(
                    lane == 0,
                    pltpu.roll(mixed, LANES - 16 - c, 1),
                    pltpu.roll(mixed, LANES - 1 - c, 1),
                )

        def advance(ch, sums, sweep=sweep, last=last, old=old):
            @pl.when(me < n - 1)
            def _():
                down_copy(sweep, ch).wait_recv()

            @pl.when(me > 0)
            def _():
                up_copy(sweep, ch).wait_recv()

            for part in range(span // GROUP):
                at = pl.multiple_of(2 * (ch * span + part * GROUP), 2 * GROUP)
                piece = slice(part * GROUP, (part + 1) * GROUP)
                for r in range(2):
                    def near(offset):
                        return [
                            old[c, pl.ds(PAD + at + r + offset, GROUP, stride=2), :]
                            for c in range(comps)
                        ]

                    def here(ref, c):
                        return ref[c, pl.ds(at + r, GROUP, stride=2), :]

                    centre, before, after = near(0), near(-2), near(2)
                    if r == 0:
                        below = [
                            jnp.where(below_ok, rcv_lo[sweep, ch, c, piece, :].astype(f32), 0.0)
                            for c in range(comps)
                        ]
                        above = near(1)
                    else:
                        below = near(-1)
                        above = [
                            jnp.where(above_ok, rcv_hi[sweep, ch, c, piece, :].astype(f32), 0.0)
                            for c in range(comps)
                        ]
                    fore = [
                        jnp.where(lane == 0, ghost[sweep, r, c], pltpu.roll(centre[c], 1, 1))
                        for c in range(comps)
                    ]
                    aft = [
                        jnp.where(
                            lane == LANES - 1, ghost[sweep, r, c],
                            pltpu.roll(centre[c], LANES - 1, 1),
                        )
                        for c in range(comps)
                    ]
                    values = update(
                        centre, before, after, below, above, fore, aft,
                        [here(prim, c) for c in range(6)],
                        [here(src, c) for c in range(comps)],
                        ps[pl.ds(at + r, GROUP, stride=2), :],
                    )
                    for c in range(comps):
                        if last:
                            fin[c, pl.ds(at + r, GROUP, stride=2), :] = values[c]
                        else:
                            mid[c, pl.ds(PAD + at + r, GROUP, stride=2), :] = values[c]
                            target = (snd_dn, snd_up)[r]
                            target[sweep + 1, ch, c, piece, :] = values[c].astype(HALO)
                    if not last:
                        sums = added(sums, r, values)
            if last:
                store(ch).start()
            else:
                send_halo(sweep + 1, ch)
            return sums

        def store(ch):
            at = pl.ds(pl.multiple_of(2 * span * ch, 2 * span), 2 * span)
            return pltpu.make_async_copy(fin.at[:, at, :], out.at[:, at, :], store_sem.at[ch])

        sums = lax.fori_loop(0, chunks, advance, () if last else zero_sums)
        if not last:
            send_sums(sweep + 1, split(sums))
            for k in range(1, n):
                sums_copy(sweep + 1, k).start()
            wrap(mid)

    def finish(ch, carry):
        for sweep in range(SWEEPS):
            @pl.when(me > 0)
            def _():
                down_copy(sweep, ch).wait_send()

            @pl.when(me < n - 1)
            def _():
                up_copy(sweep, ch).wait_send()
        store(ch).wait()
        return carry

    lax.fori_loop(0, chunks, finish, 0)
    for sweep in range(SWEEPS):
        for k in range(1, n):
            sums_copy(sweep, k).wait_send()


def on_device(n, chunks, adjoint_start, source, state, pseudo_step, row_counts):
    comps, pitch, rad, lanes = adjoint_start.shape
    cells = pitch * rad
    span = pitch // chunks
    flat = (comps, cells, lanes)
    f32 = jnp.float32
    hbm = pl.BlockSpec(memory_space=pl.ANY)
    dma = pltpu.SemaphoreType.DMA
    padded = (comps, cells + 2 * PAD, lanes)
    halo = (SWEEPS, chunks, comps, span, lanes)
    result = pl.pallas_call(
        functools.partial(kernel, n, comps, pitch, chunks),
        out_shape=jax.ShapeDtypeStruct(flat, f32),
        in_specs=[pl.BlockSpec(memory_space=pltpu.SMEM), hbm, hbm, hbm, hbm],
        out_specs=hbm,
        scratch_shapes=[
            pltpu.VMEM(padded, f32),
            pltpu.VMEM(flat, f32),
            pltpu.VMEM(flat, jnp.bfloat16),
            pltpu.VMEM((cells, lanes), f32),
            pltpu.VMEM((6, cells, lanes), f32),
            pltpu.VMEM(padded, f32),
            pltpu.VMEM(flat, f32),
            pltpu.VMEM(halo, HALO),
            pltpu.VMEM(halo, HALO),
            pltpu.VMEM(halo, HALO),
            pltpu.VMEM(halo, HALO),
            pltpu.VMEM((SWEEPS, 1, lanes), f32),
            pltpu.VMEM((SWEEPS, n, 1, lanes), f32),
            pltpu.VMEM((SWEEPS, 2, comps, 1, lanes), f32),
            pltpu.VMEM((2, n, lanes), f32),
            dma((4,)),
            dma((chunks,)),
            dma((SWEEPS, chunks)),
            dma((SWEEPS, chunks)),
            dma((SWEEPS, chunks)),
            dma((SWEEPS, chunks)),
            dma((SWEEPS, n)),
            dma((SWEEPS, n)),
        ],
        compiler_params=pltpu.CompilerParams(
            collective_id=0, has_side_effects=True, vmem_limit_bytes=32 * 1024 * 1024
        ),
    )(
        row_counts,
        adjoint_start.reshape(flat),
        source.reshape(flat),
        state.reshape(flat),
        pseudo_step.reshape(cells, lanes),
    )
    return result.reshape(adjoint_start.shape)


def solution(mesh):
    return jax.shard_map(
        functools.partial(on_device, mesh.shape["dom"], 8),
        mesh=mesh,
        in_specs=(
            P(None, None, ("groups", "dom"), None),
            P(None, None, ("groups", "dom"), None),
            P(None, None, ("groups", "dom"), None),
            P(None, ("groups", "dom"), None),
            P("groups"),
        ),
        out_specs=P(None, None, ("groups", "dom"), None),
        check_vma=False,
    )
```

```python
import functools

import jax
import jax.numpy as jnp
from jax import lax
from jax.experimental import pallas as pl
from jax.experimental.pallas import tpu as pltpu
from jax.sharding import PartitionSpec as P

BANDS = 256
ROWS = 6
SWEEPS = 2
LANES = 128
PAD = 8
GROUP = 16
MESH = pl.DeviceIdType.MESH
HALO = jnp.bfloat16
STEEP = 83.0
CHUNKS = 8


def total(parts):
    result = parts[0]
    for part in parts[1:]:
        result = result + part
    return result


def encode(values):
    peak = jnp.abs(values[0])
    for value in values[1:]:
        peak = jnp.maximum(peak, jnp.abs(value))
    peak = peak.astype(HALO)
    factor = STEEP / jnp.maximum(peak.astype(jnp.float32), 1e-30)
    return [jnp.exp(value * factor).astype(HALO) for value in values] + [peak]


def decode(codes):
    codes = [code.astype(jnp.float32) for code in codes]
    factor = jnp.maximum(codes[-1], 1e-30) * (1.0 / STEEP)
    return [jnp.log(code) * factor for code in codes[:-1]]


def update(c, pm, pp, lo, hi, am, ap, prim, source, step):
    v, enthalpy, ratio, kinetic = prim[:3], prim[3], prim[4], prim[5]
    comps = range(len(c))
    a = [
        [pm[i] - pp[i] for i in comps],
        [lo[i] - hi[i] for i in comps],
        [am[i] - ap[i] for i in comps],
    ]
    by_velocity = [
        total([a[d][1 + k] * v[k] for k in range(3)]) + a[d][4] * enthalpy + a[d][5] * ratio
        for d in range(3)
    ]
    energy = total([a[d][4] * v[d] for d in range(3)])
    by_pressure = a[0][1] + a[1][2] + a[2][3] + energy
    scaled = 0.4 * by_pressure
    convected = [kinetic * by_pressure - total([v[d] * by_velocity[d] for d in range(3)])]
    for k in range(3):
        convected.append(
            a[k][0]
            + total([a[d][1 + k] * v[d] for d in range(3)])
            - v[k] * scaled
            + by_velocity[k]
        )
    convected.append(energy + scaled)
    convected.append(total([a[d][5] * v[d] for d in range(3)]))
    result = []
    for i in comps:
        around = (pm[i] + pp[i]) + (lo[i] + hi[i]) + (am[i] + ap[i])
        image = 0.5 * convected[i] + (6.0 * c[i] - around)
        result.append(c[i] - step * (image - source[i]))
    return result


def kernel(
    n, comps, pitch, chunks,
    counts_in, adj_in, src_in, st_in, ps_in, out,
    counts, adj, src, st, ps, prim, mid,
    snd_dn, snd_up, rcv_lo, rcv_hi, gsend, gath, ghost, weight,
    load_sem, dn_send, dn_recv, up_send, up_recv, g_send, g_recv,
):
    cells = 2 * pitch
    span = pitch // chunks
    me = lax.axis_index("dom")
    f32 = jnp.float32

    loads = [
        pltpu.make_async_copy(adj_in, adj.at[:, pl.ds(PAD, cells), :], load_sem.at[0]),
        pltpu.make_async_copy(st_in, st, load_sem.at[1]),
        pltpu.make_async_copy(src_in, src, load_sem.at[2]),
        pltpu.make_async_copy(ps_in, ps, load_sem.at[3]),
        pltpu.make_async_copy(counts_in, counts, load_sem.at[4]),
    ]
    for load in loads:
        load.start()

    barrier = pltpu.get_barrier_semaphore()
    for k in range(1, n):
        pl.semaphore_signal(
            barrier, inc=1, device_id={"dom": lax.rem(me + k, n)}, device_id_type=MESH
        )

    lane = lax.broadcasted_iota(jnp.int32, (1, LANES), 1)

    def send_sums(sweep, sums):
        message = jnp.zeros((1, LANES), f32)
        for r in range(2):
            for c in range(comps):
                whole = jnp.sum(sums[r][c], axis=0, keepdims=True)
                at = c + 8 * r
                message = jnp.where(lane == at, pltpu.roll(whole, at, 1) if at else whole, message)
                message = jnp.where(lane == at + 16, pltpu.roll(whole, at + 17, 1), message)
        gsend[sweep] = message
        gath[sweep, 0] = message

    def sums_copy(sweep, k):
        return pltpu.make_async_remote_copy(
            src_ref=gsend.at[sweep],
            dst_ref=gath.at[sweep, k],
            send_sem=g_send.at[sweep, k],
            recv_sem=g_recv.at[sweep, k],
            device_id={"dom": lax.rem(me + k, n)},
            device_id_type=MESH,
        )

    def down_copy(sweep, ch):
        return pltpu.make_async_remote_copy(
            src_ref=snd_dn.at[sweep, ch],
            dst_ref=rcv_hi.at[sweep, ch],
            send_sem=dn_send.at[sweep, ch],
            recv_sem=dn_recv.at[sweep, ch],
            device_id={"dom": jnp.maximum(me - 1, 0)},
            device_id_type=MESH,
        )

    def up_copy(sweep, ch):
        return pltpu.make_async_remote_copy(
            src_ref=snd_up.at[sweep, ch],
            dst_ref=rcv_lo.at[sweep, ch],
            send_sem=up_send.at[sweep, ch],
            recv_sem=up_recv.at[sweep, ch],
            device_id={"dom": jnp.minimum(me + 1, n - 1)},
            device_id_type=MESH,
        )

    def send_halo(sweep, ch):
        @pl.when(me > 0)
        def _():
            down_copy(sweep, ch).start()

        @pl.when(me < n - 1)
        def _():
            up_copy(sweep, ch).start()

    def wrap(field):
        field[:, PAD - 2 : PAD, :] = field[:, PAD + cells - 2 : PAD + cells, :]
        field[:, PAD + cells : PAD + cells + 2, :] = field[:, PAD : PAD + 2, :]

    zero_sums = tuple(jnp.zeros((8, LANES), f32) for _ in range(2 * comps))

    def added(sums, r, values):
        sums = list(sums)
        for c in range(comps):
            for part in range(GROUP // 8):
                sums[r * comps + c] = sums[r * comps + c] + values[c][8 * part : 8 * part + 8]
        return tuple(sums)

    def split(sums):
        return [sums[:comps], sums[comps:]]

    loads[0].wait()

    def first(ch, sums):
        for part in range(span // GROUP):
            at = pl.multiple_of(PAD + 2 * (ch * span + part * GROUP), 8)
            for r in range(2):
                values = [
                    adj[c, pl.ds(at + r, GROUP, stride=2), :] for c in range(comps)
                ]
                target = (snd_dn, snd_up)[r]
                for c, code in enumerate(encode(values)):
                    target[0, ch, c, part * GROUP : (part + 1) * GROUP, :] = code
                sums = added(sums, r, values)
        return sums

    sums = lax.fori_loop(0, chunks, first, zero_sums)
    send_sums(0, split(sums))
    pl.semaphore_wait(barrier, n - 1)
    for k in range(1, n):
        sums_copy(0, k).start()

    def send_first(ch, carry):
        send_halo(0, ch)
        return carry

    lax.fori_loop(0, chunks, send_first, 0)
    wrap(adj)

    loads[4].wait()
    starts, ends = [], []
    end = jnp.int32(0)
    for r in range(ROWS):
        starts.append(end)
        end = end + counts[r]
        ends.append(end)

    def placed(dev):
        row = total([(dev >= e).astype(jnp.int32) for e in ends])
        start = jnp.zeros_like(row)
        count = jnp.zeros_like(row)
        for r in range(ROWS):
            start = jnp.where(row == r, starts[r], start)
            count = jnp.where(row == r, counts[r], count)
        return row, start, count

    band = lax.broadcasted_iota(jnp.int32, (1, BANDS), 1)

    def overlap(position, row_cells):
        low = jnp.maximum(position * BANDS, band * row_cells)
        high = jnp.minimum((position + 1) * BANDS, (band + 1) * row_cells)
        return jnp.maximum(high - low, 0).astype(f32)

    mine = jnp.full((1, 1), me, jnp.int32)
    my_row, my_start, my_count = placed(mine)
    dev = me - lax.broadcasted_iota(jnp.int32, (n, 1), 0)
    dev = jnp.where(dev < 0, dev + n, dev)
    row, start, count = placed(dev)
    from_next = (row == my_row + 1).astype(f32)
    from_prev = (row == my_row - 1).astype(f32)
    own = [overlap(2 * (mine - my_start) + i, 2 * my_count) for i in range(2)]
    theirs = [overlap(2 * (dev - start) + r, 2 * count) for r in range(2)]
    scale = 1.0 / (pitch * BANDS * 2 * count).astype(f32)
    for i in range(2):
        dots = [jnp.sum(theirs[r] * own[i], axis=1, keepdims=True) * scale for r in range(2)]
        weight[i] = jnp.where(
            lane < 8, from_next * dots[0],
            jnp.where(
                lane < 16, from_next * dots[1],
                jnp.where(
                    lane < 24, from_prev * dots[0],
                    jnp.where(lane < 32, from_prev * dots[1], 0.0),
                ),
            ),
        )

    place = jnp.zeros((1, LANES), jnp.int32) + (mine - my_start)
    below_ok = place > 0
    above_ok = place + 1 < my_count

    loads[1].wait()

    def primitive(j, carry):
        at = pl.ds(pl.multiple_of(j * 16, 16), 16)
        flow = [st[c, at, :].astype(f32) for c in range(6)]
        inverse = 1.0 / flow[0]
        v = [flow[1 + d] * inverse for d in range(3)]
        kinetic = 0.5 * total([flow[1 + d] * v[d] for d in range(3)])
        pressure = 0.4 * (flow[4] - kinetic)
        values = v + [(flow[4] + pressure) * inverse, flow[5] * inverse, 0.4 * kinetic * inverse]
        for c in range(6):
            prim[c, at, :] = values[c]
        return carry

    lax.fori_loop(0, cells // 16, primitive, 0)
    loads[2].wait()
    loads[3].wait()

    def make_ghosts(sweep):
        for k in range(1, n):
            sums_copy(sweep, k).wait_recv()
        gathered = gath[sweep][:, 0, :]
        for i in range(2):
            mixed = jnp.sum(weight[i] * gathered, axis=0, keepdims=True)
            mixed = mixed + pltpu.roll(mixed, LANES - 8, 1)
            for c in range(comps):
                ghost[i, c] = jnp.where(
                    lane == 0,
                    pltpu.roll(mixed, LANES - 16 - c, 1),
                    jnp.where(lane == LANES - 1, pltpu.roll(mixed, LANES - 1 - c, 1), 0.0),
                )

    for sweep in range(SWEEPS):
        last = sweep == SWEEPS - 1
        old = adj if sweep == 0 else mid
        if not last:
            make_ghosts(sweep)

        def advance(ch, sums, sweep=sweep, last=last, old=old):
            @pl.when(me < n - 1)
            def _():
                down_copy(sweep, ch).wait_recv()

            @pl.when(me > 0)
            def _():
                up_copy(sweep, ch).wait_recv()

            for part in range(span // GROUP):
                at = pl.multiple_of(2 * (ch * span + part * GROUP), 2 * GROUP)
                piece = slice(part * GROUP, (part + 1) * GROUP)
                for r in range(2):
                    def near(offset):
                        return [
                            old[c, pl.ds(PAD + at + r + offset, GROUP, stride=2), :]
                            for c in range(comps)
                        ]

                    def here(ref, c):
                        return ref[c, pl.ds(at + r, GROUP, stride=2), :]

                    centre, before, after = near(0), near(-2), near(2)
                    if r == 0:
                        codes = [rcv_lo[sweep, ch, c, piece, :] for c in range(comps + 1)]
                        below = [jnp.where(below_ok, value, 0.0) for value in decode(codes)]
                        above = near(1)
                    else:
                        below = near(-1)
                        codes = [rcv_hi[sweep, ch, c, piece, :] for c in range(comps + 1)]
                        above = [jnp.where(above_ok, value, 0.0) for value in decode(codes)]
                    fore = [
                        jnp.where(lane == 0, 0.0 if last else ghost[r, c], pltpu.roll(centre[c], 1, 1))
                        for c in range(comps)
                    ]
                    aft = [
                        jnp.where(
                            lane == LANES - 1, 0.0 if last else ghost[r, c],
                            pltpu.roll(centre[c], LANES - 1, 1),
                        )
                        for c in range(comps)
                    ]
                    values = update(
                        centre, before, after, below, above, fore, aft,
                        [here(prim, c) for c in range(6)],
                        [here(src, c) for c in range(comps)],
                        ps[pl.ds(at + r, GROUP, stride=2), :],
                    )
                    for c in range(comps):
                        if last:
                            out[c, pl.ds(at + r, GROUP, stride=2), :] = values[c]
                        else:
                            mid[c, pl.ds(PAD + at + r, GROUP, stride=2), :] = values[c]
                    if not last:
                        target = (snd_dn, snd_up)[r]
                        for c, code in enumerate(encode(values)):
                            target[sweep + 1, ch, c, piece, :] = code
                        sums = added(sums, r, values)
            if not last:
                send_halo(sweep + 1, ch)
            return sums

        sums = lax.fori_loop(0, chunks, advance, () if last else zero_sums)
        if not last:
            send_sums(sweep + 1, split(sums))
            for k in range(1, n):
                sums_copy(sweep + 1, k).start()
            wrap(mid)

    make_ghosts(SWEEPS - 1)
    odd = lax.broadcasted_iota(jnp.int32, (8, LANES), 0) % 2 == 1
    around = [jnp.where(odd, ghost[1, c], ghost[0, c]) for c in range(comps)]
    cross = [jnp.where(lane == 0, value, -value) for value in around]

    def correct(j, carry):
        for part in range(2):
            at = pl.ds(pl.multiple_of(j * 16, 16) + 8 * part, 8)
            v = [prim[k, at, :] for k in range(3)]
            by_velocity = (
                total([cross[1 + k] * v[k] for k in range(3)])
                + cross[4] * prim[3, at, :] + cross[5] * prim[4, at, :]
            )
            energy = cross[4] * v[2]
            by_pressure = cross[3] + energy
            scaled = 0.4 * by_pressure
            convected = [
                prim[5, at, :] * by_pressure - v[2] * by_velocity,
                cross[1] * v[2] - v[0] * scaled,
                cross[2] * v[2] - v[1] * scaled,
                cross[0] + cross[3] * v[2] - v[2] * scaled + by_velocity,
                energy + scaled,
                cross[5] * v[2],
            ]
            for c in range(comps):
                out[c, at, :] = out[c, at, :] - ps[at, :] * (0.5 * convected[c] - around[c])
        return carry

    lax.fori_loop(0, cells // 16, correct, 0)

    def finish(ch, carry):
        for sweep in range(SWEEPS):
            @pl.when(me > 0)
            def _():
                down_copy(sweep, ch).wait_send()

            @pl.when(me < n - 1)
            def _():
                up_copy(sweep, ch).wait_send()
        return carry

    lax.fori_loop(0, chunks, finish, 0)
    for sweep in range(SWEEPS):
        for k in range(1, n):
            sums_copy(sweep, k).wait_send()


def on_device(n, chunks, adjoint_start, source, state, pseudo_step, row_counts):
    comps, pitch, rad, lanes = adjoint_start.shape
    cells = pitch * rad
    span = pitch // chunks
    flat = (comps, cells, lanes)
    f32 = jnp.float32
    hbm = pl.BlockSpec(memory_space=pltpu.HBM)
    dma = pltpu.SemaphoreType.DMA
    padded = (comps, cells + 2 * PAD, lanes)
    halo = (SWEEPS, chunks, comps + 1, span, lanes)
    result = pl.pallas_call(
        functools.partial(kernel, n, comps, pitch, chunks),
        out_shape=pltpu.VMEM(flat, f32),
        in_specs=[hbm] * 5,
        out_specs=pl.BlockSpec(memory_space=pltpu.VMEM),
        scratch_shapes=[
            pltpu.SMEM((ROWS,), jnp.int32),
            pltpu.VMEM(padded, f32),
            pltpu.VMEM(flat, f32),
            pltpu.VMEM(flat, jnp.bfloat16),
            pltpu.VMEM((cells, lanes), f32),
            pltpu.VMEM((6, cells, lanes), f32),
            pltpu.VMEM(padded, f32),
            pltpu.VMEM(halo, HALO),
            pltpu.VMEM(halo, HALO),
            pltpu.VMEM(halo, HALO),
            pltpu.VMEM(halo, HALO),
            pltpu.VMEM((SWEEPS, 1, lanes), f32),
            pltpu.VMEM((SWEEPS, n, 1, lanes), f32),
            pltpu.VMEM((2, comps, 1, lanes), f32),
            pltpu.VMEM((2, n, lanes), f32),
            dma((5,)),
            dma((SWEEPS, chunks)),
            dma((SWEEPS, chunks)),
            dma((SWEEPS, chunks)),
            dma((SWEEPS, chunks)),
            dma((SWEEPS, n)),
            dma((SWEEPS, n)),
        ],
        compiler_params=pltpu.CompilerParams(
            collective_id=0, has_side_effects=True, vmem_limit_bytes=60 * 1024 * 1024
        ),
    )(
        row_counts,
        adjoint_start.reshape(flat),
        source.reshape(flat),
        state.reshape(flat),
        pseudo_step.reshape(cells, lanes),
    )
    return result.reshape(adjoint_start.shape)


def solution(mesh):
    return jax.shard_map(
        functools.partial(on_device, mesh.shape["dom"], CHUNKS),
        mesh=mesh,
        in_specs=(
            P(None, None, ("groups", "dom"), None),
            P(None, None, ("groups", "dom"), None),
            P(None, None, ("groups", "dom"), None),
            P(None, ("groups", "dom"), None),
            P("groups"),
        ),
        out_specs=P(None, None, ("groups", "dom"), None),
        check_vma=False,
    )
```

```python
import functools

import jax
import jax.numpy as jnp
from jax import lax
from jax.experimental import pallas as pl
from jax.experimental.pallas import tpu as pltpu
from jax.sharding import PartitionSpec as P

BANDS = 256
ROWS = 6
SWEEPS = 2
LANES = 128
PAD = 8
GROUP = 16
MESH = pl.DeviceIdType.MESH
HALO = jnp.bfloat16
STEEP = 83.0
CHUNKS = 4


def total(parts):
    result = parts[0]
    for part in parts[1:]:
        result = result + part
    return result


def encode(values):
    peak = jnp.abs(values[0])
    for value in values[1:]:
        peak = jnp.maximum(peak, jnp.abs(value))
    peak = peak.astype(HALO)
    factor = STEEP / jnp.maximum(peak.astype(jnp.float32), 1e-30)
    return [jnp.exp(value * factor).astype(HALO) for value in values] + [peak]


def decode(codes):
    codes = [code.astype(jnp.float32) for code in codes]
    factor = jnp.maximum(codes[-1], 1e-30) * (1.0 / STEEP)
    return [jnp.log(code) * factor for code in codes[:-1]]


def update(c, pm, pp, lo, hi, am, ap, prim, source, step):
    v, enthalpy, ratio, kinetic = prim[:3], prim[3], prim[4], prim[5]
    comps = range(len(c))
    a = [
        [pm[i] - pp[i] for i in comps],
        [lo[i] - hi[i] for i in comps],
        [am[i] - ap[i] for i in comps],
    ]
    by_velocity = [
        total([a[d][1 + k] * v[k] for k in range(3)]) + a[d][4] * enthalpy + a[d][5] * ratio
        for d in range(3)
    ]
    energy = total([a[d][4] * v[d] for d in range(3)])
    by_pressure = a[0][1] + a[1][2] + a[2][3] + energy
    scaled = 0.4 * by_pressure
    convected = [kinetic * by_pressure - total([v[d] * by_velocity[d] for d in range(3)])]
    for k in range(3):
        convected.append(
            a[k][0]
            + total([a[d][1 + k] * v[d] for d in range(3)])
            - v[k] * scaled
            + by_velocity[k]
        )
    convected.append(energy + scaled)
    convected.append(total([a[d][5] * v[d] for d in range(3)]))
    result = []
    for i in comps:
        around = (pm[i] + pp[i]) + (lo[i] + hi[i]) + (am[i] + ap[i])
        image = 0.5 * convected[i] + (6.0 * c[i] - around)
        result.append(c[i] - step * (image - source[i]))
    return result


def kernel(
    n, comps, pitch, chunks,
    counts_in, adj_in, src_in, st_in, ps_in, out,
    counts, adj, src, st, ps, prim, mid,
    snd_dn, snd_up, rcv_lo, rcv_hi, gsend, gath, ghost, weight,
    load_sem, dn_send, dn_recv, up_send, up_recv, g_send, g_recv,
):
    cells = 2 * pitch
    span = pitch // chunks
    me = lax.axis_index("dom")
    f32 = jnp.float32

    loads = [
        pltpu.make_async_copy(adj_in, adj.at[:, pl.ds(PAD, cells), :], load_sem.at[0]),
        pltpu.make_async_copy(st_in, st, load_sem.at[1]),
        pltpu.make_async_copy(src_in, src, load_sem.at[2]),
        pltpu.make_async_copy(ps_in, ps, load_sem.at[3]),
        pltpu.make_async_copy(counts_in, counts, load_sem.at[4]),
    ]
    for load in loads:
        load.start()

    barrier = pltpu.get_barrier_semaphore()
    for k in range(1, n):
        pl.semaphore_signal(
            barrier, inc=1, device_id={"dom": lax.rem(me + k, n)}, device_id_type=MESH
        )

    lane = lax.broadcasted_iota(jnp.int32, (1, LANES), 1)

    def send_sums(sweep, sums):
        message = jnp.zeros((1, LANES), f32)
        for r in range(2):
            for c in range(comps):
                whole = jnp.sum(sums[r][c], axis=0, keepdims=True)
                at = c + 8 * r
                message = jnp.where(lane == at, pltpu.roll(whole, at, 1) if at else whole, message)
                message = jnp.where(lane == at + 16, pltpu.roll(whole, at + 17, 1), message)
        gsend[sweep] = message
        gath[sweep, 0] = message

    def sums_copy(sweep, k):
        return pltpu.make_async_remote_copy(
            src_ref=gsend.at[sweep],
            dst_ref=gath.at[sweep, k],
            send_sem=g_send.at[sweep, k],
            recv_sem=g_recv.at[sweep, k],
            device_id={"dom": lax.rem(me + k, n)},
            device_id_type=MESH,
        )

    def down_copy(sweep, ch):
        return pltpu.make_async_remote_copy(
            src_ref=snd_dn.at[sweep, ch],
            dst_ref=rcv_hi.at[sweep, ch],
            send_sem=dn_send.at[sweep, ch],
            recv_sem=dn_recv.at[sweep, ch],
            device_id={"dom": jnp.maximum(me - 1, 0)},
            device_id_type=MESH,
        )

    def up_copy(sweep, ch):
        return pltpu.make_async_remote_copy(
            src_ref=snd_up.at[sweep, ch],
            dst_ref=rcv_lo.at[sweep, ch],
            send_sem=up_send.at[sweep, ch],
            recv_sem=up_recv.at[sweep, ch],
            device_id={"dom": jnp.minimum(me + 1, n - 1)},
            device_id_type=MESH,
        )

    def send_halo(sweep, ch):
        @pl.when(me > 0)
        def _():
            down_copy(sweep, ch).start()

        @pl.when(me < n - 1)
        def _():
            up_copy(sweep, ch).start()

    def wrap(field):
        field[:, PAD - 2 : PAD, :] = field[:, PAD + cells - 2 : PAD + cells, :]
        field[:, PAD + cells : PAD + cells + 2, :] = field[:, PAD : PAD + 2, :]

    zero_sums = tuple(jnp.zeros((8, LANES), f32) for _ in range(2 * comps))

    def added(sums, r, values):
        sums = list(sums)
        for c in range(comps):
            for part in range(GROUP // 8):
                sums[r * comps + c] = sums[r * comps + c] + values[c][8 * part : 8 * part + 8]
        return tuple(sums)

    def split(sums):
        return [sums[:comps], sums[comps:]]

    def put_halo(sweep, ch, field):
        at = pl.multiple_of(PAD + 2 * ch * span, 8)
        for r, target in ((0, snd_dn), (1, snd_up)):
            codes = encode([
                field[c, pl.ds(at + r + 2 * GROUP * part, GROUP, stride=2), :]
                for part in range(span // GROUP) for c in range(comps)
            ])
            for k, code in enumerate(codes):
                target[sweep, ch, k] = code

    loads[0].wait()

    def first(ch, sums):
        for part in range(span // GROUP):
            at = pl.multiple_of(PAD + 2 * (ch * span + part * GROUP), 8)
            for r in range(2):
                values = [
                    adj[c, pl.ds(at + r, GROUP, stride=2), :] for c in range(comps)
                ]
                sums = added(sums, r, values)
        put_halo(0, ch, adj)
        return sums

    sums = lax.fori_loop(0, chunks, first, zero_sums)
    send_sums(0, split(sums))
    pl.semaphore_wait(barrier, n - 1)
    send_halo(0, 0)
    for k in range(1, n):
        sums_copy(0, k).start()

    def send_first(ch, carry):
        send_halo(0, ch)
        return carry

    lax.fori_loop(1, chunks, send_first, 0)
    wrap(adj)

    loads[4].wait()
    starts, ends = [], []
    end = jnp.int32(0)
    for r in range(ROWS):
        starts.append(end)
        end = end + counts[r]
        ends.append(end)

    def placed(dev):
        row = total([(dev >= e).astype(jnp.int32) for e in ends])
        start = jnp.zeros_like(row)
        count = jnp.zeros_like(row)
        for r in range(ROWS):
            start = jnp.where(row == r, starts[r], start)
            count = jnp.where(row == r, counts[r], count)
        return row, start, count

    band = lax.broadcasted_iota(jnp.int32, (1, BANDS), 1)

    def overlap(position, row_cells):
        low = jnp.maximum(position * BANDS, band * row_cells)
        high = jnp.minimum((position + 1) * BANDS, (band + 1) * row_cells)
        return jnp.maximum(high - low, 0).astype(f32)

    mine = jnp.full((1, 1), me, jnp.int32)
    my_row, my_start, my_count = placed(mine)
    dev = me - lax.broadcasted_iota(jnp.int32, (n, 1), 0)
    dev = jnp.where(dev < 0, dev + n, dev)
    row, start, count = placed(dev)
    from_next = (row == my_row + 1).astype(f32)
    from_prev = (row == my_row - 1).astype(f32)
    own = [overlap(2 * (mine - my_start) + i, 2 * my_count) for i in range(2)]
    theirs = [overlap(2 * (dev - start) + r, 2 * count) for r in range(2)]
    scale = 1.0 / (pitch * BANDS * 2 * count).astype(f32)
    for i in range(2):
        dots = [jnp.sum(theirs[r] * own[i], axis=1, keepdims=True) * scale for r in range(2)]
        weight[i] = jnp.where(
            lane < 8, from_next * dots[0],
            jnp.where(
                lane < 16, from_next * dots[1],
                jnp.where(
                    lane < 24, from_prev * dots[0],
                    jnp.where(lane < 32, from_prev * dots[1], 0.0),
                ),
            ),
        )

    place = jnp.zeros((1, LANES), jnp.int32) + (mine - my_start)
    below_ok = place > 0
    above_ok = place + 1 < my_count

    loads[1].wait()

    def primitive(j, carry):
        at = pl.ds(pl.multiple_of(j * 16, 16), 16)
        flow = [st[c, at, :].astype(f32) for c in range(6)]
        inverse = 1.0 / flow[0]
        v = [flow[1 + d] * inverse for d in range(3)]
        kinetic = 0.5 * total([flow[1 + d] * v[d] for d in range(3)])
        pressure = 0.4 * (flow[4] - kinetic)
        values = v + [(flow[4] + pressure) * inverse, flow[5] * inverse, 0.4 * kinetic * inverse]
        for c in range(6):
            prim[c, at, :] = values[c]
        return carry

    lax.fori_loop(0, cells // 16, primitive, 0)
    loads[2].wait()
    loads[3].wait()

    def make_ghosts(sweep):
        for k in range(1, n):
            sums_copy(sweep, k).wait_recv()
        gathered = gath[sweep][:, 0, :]
        for i in range(2):
            mixed = jnp.sum(weight[i] * gathered, axis=0, keepdims=True)
            mixed = mixed + pltpu.roll(mixed, LANES - 8, 1)
            for c in range(comps):
                ghost[i, c] = jnp.where(
                    lane == 0,
                    pltpu.roll(mixed, LANES - 16 - c, 1),
                    jnp.where(lane == LANES - 1, pltpu.roll(mixed, LANES - 1 - c, 1), 0.0),
                )

    for sweep in range(SWEEPS):
        last = sweep == SWEEPS - 1
        old = adj if sweep == 0 else mid
        if not last:
            make_ghosts(sweep)

        def advance(ch, sums, sweep=sweep, last=last, old=old, early=last):
            @pl.when(me < n - 1)
            def _():
                down_copy(sweep, ch).wait_recv()

            @pl.when(me > 0)
            def _():
                up_copy(sweep, ch).wait_recv()

            for part in range(span // GROUP):
                at = pl.multiple_of(2 * (ch * span + part * GROUP), 2 * GROUP)

                def got(ref, part=part):
                    kept = [ref[sweep, ch, part * comps + c] for c in range(comps)]
                    return kept + [ref[sweep, ch, span // GROUP * comps]]

                for r in range(2):
                    def near(offset):
                        return [
                            old[c, pl.ds(PAD + at + r + offset, GROUP, stride=2), :]
                            for c in range(comps)
                        ]

                    def here(ref, c):
                        return ref[c, pl.ds(at + r, GROUP, stride=2), :]

                    centre, before, after = near(0), near(-2), near(2)
                    if r == 0:
                        codes = got(rcv_lo)
                        below = [jnp.where(below_ok, value, 0.0) for value in decode(codes)]
                        above = near(1)
                    else:
                        below = near(-1)
                        codes = got(rcv_hi)
                        above = [jnp.where(above_ok, value, 0.0) for value in decode(codes)]
                    fore = [
                        jnp.where(lane == 0, 0.0 if early else ghost[r, c], pltpu.roll(centre[c], 1, 1))
                        for c in range(comps)
                    ]
                    aft = [
                        jnp.where(
                            lane == LANES - 1, 0.0 if early else ghost[r, c],
                            pltpu.roll(centre[c], LANES - 1, 1),
                        )
                        for c in range(comps)
                    ]
                    values = update(
                        centre, before, after, below, above, fore, aft,
                        [here(prim, c) for c in range(6)],
                        [here(src, c) for c in range(comps)],
                        ps[pl.ds(at + r, GROUP, stride=2), :],
                    )
                    for c in range(comps):
                        if last:
                            out[c, pl.ds(at + r, GROUP, stride=2), :] = values[c]
                        else:
                            mid[c, pl.ds(PAD + at + r, GROUP, stride=2), :] = values[c]
                    if not last:
                        sums = added(sums, r, values)
            if not last:
                put_halo(sweep + 1, ch, mid)
                send_halo(sweep + 1, ch)
            return sums

        if not last:
            sums = lax.fori_loop(0, chunks, advance, zero_sums)
            send_sums(sweep + 1, split(sums))
            for k in range(1, n):
                sums_copy(sweep + 1, k).start()
            wrap(mid)
        else:
            lax.fori_loop(0, chunks - 1, advance, ())

    make_ghosts(SWEEPS - 1)
    odd = lax.broadcasted_iota(jnp.int32, (8, LANES), 0) % 2 == 1
    around = [jnp.where(odd, ghost[1, c], ghost[0, c]) for c in range(comps)]
    cross = [jnp.where(lane == 0, value, -value) for value in around]

    def correct(j, carry):
        for part in range(2):
            at = pl.ds(pl.multiple_of(j * 16, 16) + 8 * part, 8)
            v = [prim[k, at, :] for k in range(3)]
            by_velocity = (
                total([cross[1 + k] * v[k] for k in range(3)])
                + cross[4] * prim[3, at, :] + cross[5] * prim[4, at, :]
            )
            energy = cross[4] * v[2]
            by_pressure = cross[3] + energy
            scaled = 0.4 * by_pressure
            convected = [
                prim[5, at, :] * by_pressure - v[2] * by_velocity,
                cross[1] * v[2] - v[0] * scaled,
                cross[2] * v[2] - v[1] * scaled,
                cross[0] + cross[3] * v[2] - v[2] * scaled + by_velocity,
                energy + scaled,
                cross[5] * v[2],
            ]
            for c in range(comps):
                out[c, at, :] = out[c, at, :] - ps[at, :] * (0.5 * convected[c] - around[c])
        return carry

    lax.fori_loop(0, (cells - 2 * span) // 16, correct, 0)
    advance(chunks - 1, (), early=False)

    def finish(ch, carry):
        for sweep in range(SWEEPS):
            @pl.when(me > 0)
            def _():
                down_copy(sweep, ch).wait_send()

            @pl.when(me < n - 1)
            def _():
                up_copy(sweep, ch).wait_send()
        return carry

    lax.fori_loop(0, chunks, finish, 0)
    for sweep in range(SWEEPS):
        for k in range(1, n):
            sums_copy(sweep, k).wait_send()


def on_device(n, chunks, adjoint_start, source, state, pseudo_step, row_counts):
    comps, pitch, rad, lanes = adjoint_start.shape
    cells = pitch * rad
    span = pitch // chunks
    flat = (comps, cells, lanes)
    f32 = jnp.float32
    hbm = pl.BlockSpec(memory_space=pltpu.HBM)
    dma = pltpu.SemaphoreType.DMA
    padded = (comps, cells + 2 * PAD, lanes)
    halo = (SWEEPS, chunks, span // GROUP * comps + 1, GROUP, lanes)
    result = pl.pallas_call(
        functools.partial(kernel, n, comps, pitch, chunks),
        out_shape=pltpu.VMEM(flat, f32),
        in_specs=[hbm] * 5,
        out_specs=pl.BlockSpec(memory_space=pltpu.VMEM),
        scratch_shapes=[
            pltpu.SMEM((ROWS,), jnp.int32),
            pltpu.VMEM(padded, f32),
            pltpu.VMEM(flat, f32),
            pltpu.VMEM(flat, jnp.bfloat16),
            pltpu.VMEM((cells, lanes), f32),
            pltpu.VMEM((6, cells, lanes), f32),
            pltpu.VMEM(padded, f32),
            pltpu.VMEM(halo, HALO),
            pltpu.VMEM(halo, HALO),
            pltpu.VMEM(halo, HALO),
            pltpu.VMEM(halo, HALO),
            pltpu.VMEM((SWEEPS, 1, lanes), f32),
            pltpu.VMEM((SWEEPS, n, 1, lanes), f32),
            pltpu.VMEM((2, comps, 1, lanes), f32),
            pltpu.VMEM((2, n, lanes), f32),
            dma((5,)),
            dma((SWEEPS, chunks)),
            dma((SWEEPS, chunks)),
            dma((SWEEPS, chunks)),
            dma((SWEEPS, chunks)),
            dma((SWEEPS, n)),
            dma((SWEEPS, n)),
        ],
        compiler_params=pltpu.CompilerParams(
            collective_id=0, has_side_effects=True, vmem_limit_bytes=60 * 1024 * 1024
        ),
    )(
        row_counts,
        adjoint_start.reshape(flat),
        source.reshape(flat),
        state.reshape(flat),
        pseudo_step.reshape(cells, lanes),
    )
    return result.reshape(adjoint_start.shape)


def solution(mesh):
    return jax.shard_map(
        functools.partial(on_device, mesh.shape["dom"], CHUNKS),
        mesh=mesh,
        in_specs=(
            P(None, None, ("groups", "dom"), None),
            P(None, None, ("groups", "dom"), None),
            P(None, None, ("groups", "dom"), None),
            P(None, ("groups", "dom"), None),
            P("groups"),
        ),
        out_specs=P(None, None, ("groups", "dom"), None),
        check_vma=False,
    )
```
